1024 devices in a mesh: fsdp: 64 (over z, x), expert: 4 (over y_lo), dp: 4 (over y_hi, core).
Axes of the slice: x: 8, y: 8 (y_hi: 2, y_lo: 4; y = y_hi * 4 + y_lo), z: 8, core: 2. Of those that a mesh axis runs over, the one named last changes fastest.
Arguments:
- tokens: bfloat16 [128, 16, 2048], P('fsdp', ('expert', 'dp')), may hold values from -6 to 6
- cotangent: bfloat16 [128, 16, 2048], P('fsdp', ('expert', 'dp')), may hold values from -4 to 4
- expert_ids: int32 [128, 16, 2], P(None, ('expert', 'dp')), may hold values from 0 to 3, as said below
- slot_ids: int32 [128, 16, 2], P(None, ('expert', 'dp')), may hold values from -1 to 63, as said below
- route_probs: bfloat16 [128, 16, 2], P(None, ('expert', 'dp')), may hold values from 0.049804688 to 0.94921875
- gate_weight: bfloat16 [4, 2048, 8192], P('expert', None, 'fsdp'), may hold values from -0.125 to 0.125
- up_weight: bfloat16 [4, 2048, 8192], P('expert', None, 'fsdp'), may hold values from -0.125 to 0.125
- down_weight: bfloat16 [4, 8192, 2048], P('expert', 'fsdp'), may hold values from -0.0625 to 0.0625
Outputs:
- grad_gate: bfloat16 [4, 2048, 8192], P('expert', 'dp', 'fsdp')
- grad_up: bfloat16 [4, 2048, 8192], P('expert', 'dp', 'fsdp')
- grad_down: bfloat16 [4, 8192, 2048], P('expert', 'fsdp', 'dp')
- token_grad: bfloat16 [128, 16, 2048], P('fsdp', ('expert', 'dp'))
- prob_grad: float32 [128, 16, 2], P('fsdp', ('expert', 'dp'))
The draws below stay inside these ranges and needn't reach their ends.
Inputs may be any that keep to these rules, and one draw needn't show every extreme that they name: `expert_ids`: each token names two different experts. `slot_ids`: within a group, the choices of one expert get slots 0, 1, 2, ... by arrival in token order, a token's first choice before its second; a choice arriving after all 64 slots of its expert are taken gets -1 and is dropped. In every group some expert receives more than 64 choices, and it is the same expert in all groups of one dp index.
All inputs are finite; a program needn't handle non-finite values.
Results may differ from the reference program's by a relative error of at most 0.015.
Values may be sent and summed in bfloat16 or wider, within the bound.
No kernel may reach another device: no remote copies, remote signals or barrier semaphores. Data moves between devices by JAX's collectives and lax.ppermute only.
A program may use at most 32 MiB of HBM per device.

```python
import jax
import jax.numpy as jnp
from jax import lax

D = 2048
FF = 8192
EXPERTS = 4
GROUP_TOKENS = 128
GROUPS = 16
CAP = 64
N_EXPERT = 4
N_DP = 4


def route_table(key):
    folded = jax.random.fold_in(key, 4099)
    subkeys = jax.random.split(folded, 4)
    hot_expert = jax.random.randint(subkeys[0], (N_DP,), 0, EXPERTS)
    group_hot = jnp.tile(hot_expert, N_EXPERT)
    token_iota = jnp.arange(GROUP_TOKENS, dtype=jnp.int32)[:, None]
    raw_rank = jax.random.randint(subkeys[1], (GROUP_TOKENS, GROUPS), 0, 1 << 16) * GROUP_TOKENS + token_iota
    position = jnp.argsort(jnp.argsort(raw_rank, axis=0, stable=True), axis=0, stable=True)
    pinned = position < GROUP_TOKENS // 2
    uniform_pick = jax.random.randint(subkeys[2], (GROUP_TOKENS, GROUPS), 0, EXPERTS)
    leading = jnp.where(pinned, group_hot[None, :], uniform_pick)
    offset = jax.random.randint(subkeys[3], (GROUP_TOKENS, GROUPS), 1, EXPERTS)
    trailing = (leading + offset) % EXPERTS
    chosen = jnp.stack([leading, trailing], axis=-1).astype(jnp.int32)
    flattened = jnp.transpose(chosen, (0, 2, 1)).reshape(GROUP_TOKENS * 2, GROUPS)
    matches = (flattened[:, :, None] == jnp.arange(EXPERTS, dtype=jnp.int32)[None, None, :]).astype(jnp.int32)
    before = jnp.cumsum(matches, axis=0) - matches
    arrival = jnp.sum(before * matches, axis=-1)
    arrival = jnp.where(arrival < CAP, arrival, -1)
    slot_table = jnp.transpose(arrival.reshape(GROUP_TOKENS, 2, GROUPS), (0, 2, 1)).astype(jnp.int32)
    return (chosen, slot_table)


def draw_expert_ids(key, part):
    return route_table(key)[0]


def draw_slot_ids(key, part):
    return route_table(key)[1]


def levels(rng, extent, cuts, low, top_value):
    def one(axis_at, blocks):
        steps = jax.random.uniform(jax.random.fold_in(jax.random.fold_in(rng, 6), axis_at), (blocks,), jnp.float32, low / len(cuts), top_value / len(cuts))
        return jnp.repeat(jnp.exp(steps), extent[axis_at] // blocks).reshape((-1,) + (1,) * (len(extent) - axis_at - 1))

    factor_of = one(*cuts[0])
    for cut in cuts[1:]:
        factor_of = factor_of * one(*cut)
    return factor_of


def gaussian(own_key, shape, spread, limit, cuts=(), held_as=jnp.bfloat16):
    array = spread * jax.random.normal(own_key, shape, jnp.float32)
    if cuts:
        array = array * levels(own_key, shape, cuts, -0.22, 0.18)
    return jnp.clip(array, -limit, limit).astype(held_as)


def setup_inputs(seed: int = 0) -> dict:
    key_list = jax.random.split(jax.random.key(seed), 9)
    return {
        "tokens": gaussian(key_list[0], (GROUP_TOKENS, GROUPS, D), 1.0, 6.0, ((0, 64), (1, 16))),
        "cotangent": gaussian(key_list[1], (GROUP_TOKENS, GROUPS, D), 0.5, 4.0, ((0, 64), (1, 16))),
        "expert_ids": draw_expert_ids(jax.random.fold_in(key_list[8], 71), 0),
        "slot_ids": draw_slot_ids(jax.random.fold_in(key_list[8], 71), 0),
        "route_probs": jnp.clip(0.049804688 + 0.89941406 * jax.random.uniform(key_list[4], (GROUP_TOKENS, GROUPS, 2), jnp.float32) ** levels(key_list[4], (GROUP_TOKENS, GROUPS, 2), ((1, 16),), -0.2, 0.2), 0.049804688, 0.94921875).astype(jnp.bfloat16),
        "gate_weight": gaussian(key_list[5], (EXPERTS, D, FF), D ** -0.5, 0.125, ((0, 4), (2, 64))),
        "up_weight": gaussian(key_list[6], (EXPERTS, D, FF), D ** -0.5, 0.125, ((0, 4), (2, 64))),
        "down_weight": gaussian(key_list[7], (EXPERTS, FF, D), FF ** -0.5, 0.0625, ((0, 4), (1, 64))),
    }


def rounded(values):
    return lax.optimization_barrier(values.astype(jnp.bfloat16)).astype(jnp.float32)


def group_dispatch(group_x, group_dy, group_ids, group_slots, group_probs):
    total_rows = EXPERTS * CAP
    kept_slot = group_slots >= 0
    target = group_ids * CAP + jnp.where(kept_slot, group_slots, 0)
    row_iota = lax.broadcasted_iota(jnp.int32, (total_rows, GROUP_TOKENS), 0)
    leading = jnp.logical_and(row_iota == target[None, :, 0], kept_slot[None, :, 0])
    trailing = jnp.logical_and(row_iota == target[None, :, 1], kept_slot[None, :, 1])
    either = jnp.logical_or(leading, trailing).astype(jnp.bfloat16)
    sent_x = jnp.dot(either, group_x, preferred_element_type=jnp.float32).astype(jnp.bfloat16)
    sent_dy = jnp.dot(either, group_dy, preferred_element_type=jnp.float32).astype(jnp.bfloat16)
    prob_pair = group_probs.astype(jnp.float32)
    sent_prob = jnp.sum(jnp.where(leading, prob_pair[None, :, 0], 0.0) + jnp.where(trailing, prob_pair[None, :, 1], 0.0), axis=1)
    return sent_x, sent_dy, sent_prob


def regroup(values):
    trailing_dims = values.shape[2:]
    sectioned = values.reshape((N_EXPERT, N_DP, EXPERTS, CAP) + trailing_dims)
    axes_order = (2, 1, 0, 3) + tuple(range(4, 4 + len(trailing_dims)))
    return jnp.transpose(sectioned, axes_order).reshape((EXPERTS, N_DP, N_EXPERT * CAP) + trailing_dims)


def ungroup(values):
    trailing_dims = values.shape[3:]
    sectioned = values.reshape((EXPERTS, N_DP, N_EXPERT, CAP) + trailing_dims)
    axes_order = (2, 1, 0, 3) + tuple(range(4, 4 + len(trailing_dims)))
    return jnp.transpose(sectioned, axes_order).reshape((GROUPS, EXPERTS * CAP) + trailing_dims)


def expert_backward(operands):
    input_rows, upstream_rows, rows_prob, gate_matrix, up_matrix, down_matrix = operands
    grad_gate = jnp.zeros((D, FF), jnp.float32)
    grad_up = jnp.zeros((D, FF), jnp.float32)
    grad_down = jnp.zeros((FF, D), jnp.float32)
    slot_grads = []
    slot_scores = []
    for replica in range(N_DP):
        rows_x = input_rows[replica]
        rows_dy = upstream_rows[replica]
        prob_column = rows_prob[replica][:, None]
        gate_value = jnp.dot(rows_x, gate_matrix, preferred_element_type=jnp.float32)
        up_value = jnp.dot(rows_x, up_matrix, preferred_element_type=jnp.float32)
        sigmoid_gate = jax.nn.sigmoid(gate_value)
        swish_gate = gate_value * sigmoid_gate
        hidden_full = swish_gate * up_value
        hidden = hidden_full.astype(jnp.bfloat16)
        scaled = (prob_column * hidden_full).astype(jnp.bfloat16)
        back_value = jnp.dot(rows_dy, down_matrix.T, preferred_element_type=jnp.float32)
        row_score = jnp.sum(hidden.astype(jnp.float32) * back_value, axis=1)
        back_scaled = prob_column * back_value
        grad_pre = (back_scaled * up_value * sigmoid_gate * (1.0 + gate_value * (1.0 - sigmoid_gate))).astype(jnp.bfloat16)
        grad_upper = (back_scaled * swish_gate).astype(jnp.bfloat16)
        grad_gate = grad_gate + rounded(jnp.dot(rows_x.T, grad_pre, preferred_element_type=jnp.float32))
        grad_up = grad_up + rounded(jnp.dot(rows_x.T, grad_upper, preferred_element_type=jnp.float32))
        grad_down = grad_down + rounded(jnp.dot(scaled.T, rows_dy, preferred_element_type=jnp.float32))
        slot_dx = jnp.dot(grad_pre, gate_matrix.T, preferred_element_type=jnp.float32) + jnp.dot(grad_upper, up_matrix.T, preferred_element_type=jnp.float32)
        slot_grads.append(slot_dx)
        slot_scores.append(row_score)
    return (grad_gate.astype(jnp.bfloat16), grad_up.astype(jnp.bfloat16), grad_down.astype(jnp.bfloat16), jnp.stack(slot_grads), jnp.stack(slot_scores))


def group_combine(group_dx, group_score, group_ids, group_slots):
    kept_slot = group_slots >= 0
    target = (group_ids * CAP + jnp.where(kept_slot, group_slots, 0)).astype(jnp.int32)
    picked = jnp.take(group_dx, target.reshape(-1), axis=0).reshape(GROUP_TOKENS, 2, D)
    token_dx = jnp.sum(jnp.where(kept_slot[:, :, None], picked, 0.0), axis=1)
    prob_grad = jnp.where(kept_slot, jnp.take(group_score, target), 0.0)
    return token_dx, prob_grad


def reference(tokens, cotangent, expert_ids, slot_ids, route_probs, gate_weight, up_weight, down_weight):
    sent_x, sent_dy, sent_prob = jax.vmap(group_dispatch, in_axes=(1, 1, 1, 1, 1))(tokens, cotangent, expert_ids, slot_ids, route_probs)
    outcome = lax.map(expert_backward, (regroup(sent_x), regroup(sent_dy), regroup(sent_prob), gate_weight, up_weight, down_weight))
    grad_gate, grad_up, grad_down, slot_dx, slot_score = outcome
    token_dx, prob_grad = jax.vmap(group_combine, in_axes=(0, 0, 1, 1), out_axes=(1, 1))(ungroup(slot_dx), ungroup(slot_score), expert_ids, slot_ids)
    return grad_gate, grad_up, grad_down, token_dx.astype(jnp.bfloat16), prob_grad
```

```python
import jax
import jax.numpy as jnp
from jax import lax
from jax.sharding import PartitionSpec as P

BF = jnp.bfloat16
F32 = jnp.float32


def dot(a, b, ca, cb):
    return lax.dot_general(a, b, (((ca,), (cb,)), ((), ())), preferred_element_type=F32)


def shards(
    tokens, cotangent, expert_ids, slot_ids, route_probs, gate_weight, up_weight, down_weight
):
    peers = lax.axis_size("fsdp")
    experts = lax.axis_size("expert")
    me = lax.axis_index("fsdp")
    mine = lax.axis_index("expert")
    owned, _, width = tokens.shape
    feats = width // peers
    capacity = 2 * expert_ids.shape[0] // experts
    rows = experts * capacity
    hidden_units = gate_weight.shape[2]
    gate_w, up_w, down_w = gate_weight[0], up_weight[0], down_weight[0]

    own_ids = lax.dynamic_slice_in_dim(expert_ids[:, 0, :], me * owned, owned, 0)
    own_slots = lax.dynamic_slice_in_dim(slot_ids[:, 0, :], me * owned, owned, 0)
    own_probs = lax.dynamic_slice_in_dim(route_probs[:, 0, :], me * owned, owned, 0)
    cut_x = tokens[:, 0, :].reshape(owned, peers, feats)
    cut_y = cotangent[:, 0, :].reshape(owned, peers, feats)
    cut = jnp.concatenate([cut_x, cut_y], axis=2).transpose(1, 0, 2)
    cut = cut.reshape(peers, 1, owned * 2 * feats)
    routing = jnp.concatenate([own_ids.astype(BF), own_slots.astype(BF), own_probs], axis=1)
    routing = jnp.pad(routing.reshape(1, 1, owned * 6), ((0, 0), (0, 0), (0, 2 * owned * feats - 6 * owned)))
    routing = jnp.broadcast_to(routing, cut.shape)
    block = jnp.concatenate([cut, routing], axis=1)
    block = jnp.broadcast_to(block[:, None], (peers, experts, 2, 2 * owned * feats))
    block = block.reshape(peers * experts, 2, 2 * owned * feats)
    got = lax.all_to_all(block, ("fsdp", "expert"), 0, 0, tiled=True)
    got_cut, got_route = got[:, 0, :], got[:, 1, : 6 * owned].astype(F32)

    source = lax.broadcasted_iota(jnp.int32, (peers * experts, 1), 0) % experts * capacity
    row_iota = lax.broadcasted_iota(jnp.int32, (peers * experts, rows), 1)
    picks, prob_row, cut_t = [], 0.0, 0.0
    for j in range(owned):
        route = got_route[:, 6 * j : 6 * j + 6]
        first = jnp.logical_and(route[:, 0:1] == mine.astype(F32), route[:, 2:3] >= 0)
        second = jnp.logical_and(route[:, 1:2] == mine.astype(F32), route[:, 3:4] >= 0)
        slot = jnp.where(first, route[:, 2:3], route[:, 3:4]).astype(jnp.int32)
        target = jnp.where(jnp.logical_or(first, second), source + slot, -1)
        pick = row_iota == target
        prob = jnp.where(first, route[:, 4:5], route[:, 5:6])
        prob_row = prob_row + jnp.sum(jnp.where(pick, prob, 0.0), axis=0, keepdims=True)
        picks.append(pick.astype(BF))
        cut_t = cut_t + dot(got_cut[:, 2 * feats * j : 2 * feats * (j + 1)], picks[j], 0, 0)
    cut_t = jnp.broadcast_to(cut_t.astype(BF)[None], (peers, 2 * feats, rows))
    full = lax.all_to_all(cut_t, "fsdp", 0, 0, tiled=True)
    x_t = full[:, :feats].reshape(width, rows)
    y_t = full[:, feats:].reshape(width, rows)

    gate = dot(gate_w, x_t, 0, 0)
    up = dot(up_w, x_t, 0, 0)
    back = dot(down_w, y_t, 1, 0)
    sig = jax.nn.sigmoid(gate)
    swish = gate * sig
    hidden = swish * up
    scaled = (prob_row * hidden).astype(BF)
    score = jnp.sum(hidden.astype(BF).astype(F32) * back, axis=0, keepdims=True)
    scaled_back = prob_row * back
    grad_pre = (scaled_back * up * sig * (1.0 + gate * (1.0 - sig))).astype(BF)
    grad_upper = (scaled_back * swish).astype(BF)

    dx = (dot(gate_w, grad_pre, 1, 0) + dot(up_w, grad_upper, 1, 0)).astype(BF)
    dx, grad_pre, grad_upper, scaled = lax.optimization_barrier((dx, grad_pre, grad_upper, scaled))
    parts = lax.all_to_all(dx.reshape(peers, feats, rows), "fsdp", 0, 0, tiled=True)

    quarter = width // 4
    g_gate = dot(x_t, grad_pre, 1, 1).astype(BF).reshape(2, 2, quarter, hidden_units)
    g_up = dot(x_t, grad_upper, 1, 1).astype(BF).reshape(2, 2, quarter, hidden_units)
    g_down = dot(y_t, scaled, 1, 1).astype(BF).reshape(2, 2, quarter, hidden_units)
    partial = jnp.concatenate([g_gate, g_up, g_down], axis=2)
    dp = lax.axis_index("dp")
    core, half = dp % 2, dp // 2
    away = lax.dynamic_index_in_dim(partial, 1 - core, 1, keepdims=False)
    kept = lax.dynamic_index_in_dim(partial, core, 1, keepdims=False)
    near = lax.ppermute(away, "dp", [(0, 1), (1, 0), (2, 3), (3, 2)])
    both = kept.astype(F32) + near.astype(F32)
    away = lax.dynamic_index_in_dim(both, 1 - half, 0, keepdims=False).astype(BF)
    kept = lax.dynamic_index_in_dim(both, half, 0, keepdims=False)
    far = lax.ppermute(away, "dp", [(0, 2), (2, 0), (1, 3), (3, 1)])
    total = (kept + far.astype(F32)).astype(BF)
    grad_gate = total[:quarter][None]
    grad_up = total[quarter : 2 * quarter][None]
    grad_down = total[2 * quarter :].T[None]

    own_dx = jnp.sum(parts.astype(F32), axis=0).astype(BF)
    high = score.astype(BF)
    low = (score - high.astype(F32)).astype(BF)
    blank = jnp.zeros((owned * feats, rows), BF)
    returned = 0.0
    for j in range(owned):
        lead = blank[: j * feats]
        middle = blank[: (owned - 1 - j) * feats + 2 * j]
        end = blank[: owned * feats - 2 - 2 * j]
        laid = jnp.concatenate([lead, own_dx, middle, high, low, end], axis=0)
        returned = returned + dot(picks[j], laid, 1, 1)
    home = lax.all_to_all(returned.astype(BF), ("fsdp", "expert"), 0, 0, tiled=True)
    home = home.astype(F32).reshape(peers, experts, 2 * owned * feats)
    token_grad = jnp.sum(home[:, :, : owned * feats], axis=1).astype(BF)
    token_grad = token_grad.reshape(peers, owned, feats).transpose(1, 0, 2).reshape(owned, 1, width)
    scores = jnp.sum(home[:, :, owned * feats : owned * feats + 2 * owned], axis=0)
    scores = scores.reshape(experts, owned, 2).sum(axis=2)
    expert_iota = lax.broadcasted_iota(jnp.int32, (experts, owned, 2), 0)
    chosen = jnp.logical_and(expert_iota == own_ids[None], own_slots[None] >= 0)
    prob_grad = jnp.sum(jnp.where(chosen, scores[:, :, None], 0.0), axis=0)
    return grad_gate, grad_up, grad_down, token_grad, prob_grad[:, None, :]


def solution(mesh):
    return jax.shard_map(
        shards,
        mesh=mesh,
        in_specs=(
            P("fsdp", ("expert", "dp"), None),
            P("fsdp", ("expert", "dp"), None),
            P(None, ("expert", "dp"), None),
            P(None, ("expert", "dp"), None),
            P(None, ("expert", "dp"), None),
            P("expert", None, "fsdp"),
            P("expert", None, "fsdp"),
            P("expert", "fsdp", None),
        ),
        out_specs=(
            P("expert", "dp", "fsdp"),
            P("expert", "dp", "fsdp"),
            P("expert", "fsdp", "dp"),
            P("fsdp", ("expert", "dp"), None),
            P("fsdp", ("expert", "dp"), None),
        ),
        check_vma=False,
    )
```

```python
import jax
import jax.numpy as jnp
from jax import lax
from jax.sharding import PartitionSpec as P

BF = jnp.bfloat16
F32 = jnp.float32


def dot(a, b, ca, cb):
    return lax.dot_general(a, b, (((ca,), (cb,)), ((), ())), preferred_element_type=F32)


def shards(
    tokens, cotangent, expert_ids, slot_ids, route_probs, gate_weight, up_weight, down_weight
):
    peers = lax.axis_size("fsdp")
    experts = lax.axis_size("expert")
    mine = lax.axis_index("expert")
    owned, _, width = tokens.shape
    feats = width // peers
    capacity = 2 * expert_ids.shape[0] // experts
    rows = experts * capacity
    hidden_units = gate_weight.shape[2]
    gate_w, up_w, down_w = gate_weight[0], up_weight[0], down_weight[0]

    side = 1
    while side * side < peers:
        side *= 2
    xa, ya, xb, yb = feats * 4 * side // 8, feats * 3 * side // 8, feats * 4 * side // 8, feats * 5 * side // 8
    in_row = [[i * side + j for j in range(side)] for i in range(side)]
    in_column = [[i * side + j for i in range(side)] for j in range(side)]

    fields = [expert_ids[:, 0, :].astype(BF), slot_ids[:, 0, :].astype(BF), route_probs[:, 0, :]]
    fields = jnp.concatenate(fields, axis=1).reshape(peers, owned * 6)
    got_route = lax.all_gather(fields, "expert", axis=0, tiled=True).astype(F32)

    own_x, own_y = tokens[:, 0, :], cotangent[:, 0, :]
    full = (owned, side, side)
    a_x = own_x[:, : side * xa].reshape(owned, 1, side, xa)
    a_y = own_y[:, : side * ya].reshape(owned, 1, side, ya)
    b_y = own_y[:, side * ya :].reshape(owned, side, 1, yb)
    b_x = own_x[:, side * xa :].reshape(owned, side, 1, xb)
    cut = [jnp.broadcast_to(v, full + v.shape[3:]) for v in (a_x, a_y, b_y, b_x)]
    cut = jnp.concatenate(cut, axis=3).transpose(1, 2, 0, 3)
    part = xa + ya + xb + yb
    block = cut.reshape(peers, owned * part // 128, 128)
    block = jnp.broadcast_to(block[None], (experts,) + block.shape)
    block = block.reshape((experts * peers,) + block.shape[2:])
    got = lax.all_to_all(block, ("expert", "fsdp"), 0, 0, tiled=True)
    got_cut = got.reshape(experts * peers, owned, part)

    source = lax.broadcasted_iota(jnp.int32, (peers * experts, 1), 0) // peers * capacity
    row_iota = lax.broadcasted_iota(jnp.int32, (peers * experts, rows), 1)
    picks, prob_row, cut_t = [], 0.0, 0.0
    for j in range(owned):
        first_at = 6 * j
        route = got_route[:, first_at : first_at + 6]
        first = jnp.logical_and(route[:, 0:1] == mine.astype(F32), route[:, 2:3] >= 0)
        second = jnp.logical_and(route[:, 1:2] == mine.astype(F32), route[:, 3:4] >= 0)
        slot = jnp.where(first, route[:, 2:3], route[:, 3:4]).astype(jnp.int32)
        target = jnp.where(jnp.logical_or(first, second), source + slot, -1)
        pick = row_iota == target
        prob = jnp.where(first, route[:, 4:5], route[:, 5:6])
        prob_row = prob_row + jnp.sum(jnp.where(pick, prob, 0.0), axis=0, keepdims=True)
        picks.append(pick.astype(BF))
        cut_t = cut_t + dot(got_cut[:, j], picks[j], 0, 0)
    cut_t = cut_t.astype(BF)
    a_cut, b_cut = cut_t[: xa + ya], cut_t[xa + ya :]
    b_cut = jnp.broadcast_to(b_cut[None], (side,) + b_cut.shape)
    b_full = lax.all_to_all(b_cut, "fsdp", 0, 0, axis_index_groups=in_column, tiled=True)
    a_full = lax.all_gather(a_cut, "fsdp", axis=0, axis_index_groups=in_row)
    x_t = jnp.concatenate(
        [a_full[:, :xa].reshape(-1, rows), b_full[:, yb:].reshape(-1, rows)], axis=0
    )
    y_t = jnp.concatenate(
        [a_full[:, xa:].reshape(-1, rows), b_full[:, :yb].reshape(-1, rows)], axis=0
    )

    gate = dot(gate_w, x_t, 0, 0)
    up = dot(up_w, x_t, 0, 0)
    back = dot(down_w, y_t, 1, 0)
    sig = jax.nn.sigmoid(gate)
    swish = gate * sig
    hidden = swish * up
    scaled = (prob_row * hidden).astype(BF)
    score = jnp.sum(hidden.astype(BF).astype(F32) * back, axis=0, keepdims=True)
    scaled_back = prob_row * back
    grad_pre = (scaled_back * up * sig * (1.0 + gate * (1.0 - sig))).astype(BF)
    grad_upper = (scaled_back * swish).astype(BF)

    dx = (dot(gate_w, grad_pre, 1, 0) + dot(up_w, grad_upper, 1, 0)).astype(BF)
    dx, grad_pre, grad_upper, scaled = lax.optimization_barrier((dx, grad_pre, grad_upper, scaled))
    parts = lax.all_to_all(dx.reshape(peers, feats, rows), "fsdp", 0, 0, tiled=True)

    quarter = width // 4
    g_gate = dot(x_t, grad_pre, 1, 1).astype(BF).reshape(2, 2, quarter, hidden_units)
    g_up = dot(x_t, grad_upper, 1, 1).astype(BF).reshape(2, 2, quarter, hidden_units)
    g_down = dot(y_t, scaled, 1, 1).astype(BF).reshape(2, 2, quarter, hidden_units)
    partial = jnp.concatenate([g_gate, g_up, g_down], axis=2)
    dp = lax.axis_index("dp")
    core, half = dp % 2, dp // 2
    away = lax.dynamic_index_in_dim(partial, 1 - core, 1, keepdims=False)
    kept = lax.dynamic_index_in_dim(partial, core, 1, keepdims=False)
    near = lax.ppermute(away, "dp", [(0, 1), (1, 0), (2, 3), (3, 2)])
    both = kept.astype(F32) + near.astype(F32)
    away = lax.dynamic_index_in_dim(both, 1 - half, 0, keepdims=False).astype(BF)
    kept = lax.dynamic_index_in_dim(both, half, 0, keepdims=False)
    far = lax.ppermute(away, "dp", [(0, 2), (2, 0), (1, 3), (3, 1)])
    own_dx = jnp.sum(parts.astype(F32), axis=0).astype(BF)
    high = score.astype(BF)
    low = (score - high.astype(F32)).astype(BF)
    blank = jnp.zeros((owned * feats, rows), BF)
    returned = 0.0
    for j in range(owned):
        lead = blank[: j * feats]
        middle = blank[: (owned - 1 - j) * feats + 2 * j]
        end = blank[: owned * feats - 2 - 2 * j]
        laid = jnp.concatenate([lead, own_dx, middle, high, low, end], axis=0)
        returned = returned + dot(picks[j], laid, 1, 1)
    returned = returned.astype(BF)
    far, _ = lax.optimization_barrier((far, returned))
    total = (kept + far.astype(F32)).astype(BF)
    grad_gate = total[:quarter][None]
    grad_up = total[quarter : 2 * quarter][None]
    grad_down = total[2 * quarter :].T[None]
    home = lax.all_to_all(returned, ("expert", "fsdp"), 0, 0, tiled=True)
    home = home.astype(F32).reshape(experts, peers, 2 * owned * feats)
    token_grad = jnp.sum(home[:, :, : owned * feats], axis=0).astype(BF)
    token_grad = token_grad.reshape(peers, owned, feats).transpose(1, 0, 2).reshape(owned, 1, width)
    scores = jnp.sum(home[:, :, owned * feats : owned * feats + 2 * owned], axis=1)
    scores = scores.reshape(experts, owned, 2).sum(axis=2)
    me = lax.axis_index("fsdp")
    own_ids = lax.dynamic_slice_in_dim(expert_ids[:, 0, :], me * owned, owned, 0)
    own_slots = lax.dynamic_slice_in_dim(slot_ids[:, 0, :], me * owned, owned, 0)
    expert_iota = lax.broadcasted_iota(jnp.int32, (experts, owned, 2), 0)
    chosen = jnp.logical_and(expert_iota == own_ids[None], own_slots[None] >= 0)
    prob_grad = jnp.sum(jnp.where(chosen, scores[:, :, None], 0.0), axis=0)
    return grad_gate, grad_up, grad_down, token_grad, prob_grad[:, None, :]


def solution(mesh):
    return jax.shard_map(
        shards,
        mesh=mesh,
        in_specs=(
            P("fsdp", ("expert", "dp"), None),
            P("fsdp", ("expert", "dp"), None),
            P(None, ("expert", "dp"), None),
            P(None, ("expert", "dp"), None),
            P(None, ("expert", "dp"), None),
            P("expert", None, "fsdp"),
            P("expert", None, "fsdp"),
            P("expert", "fsdp", None),
        ),
        out_specs=(
            P("expert", "dp", "fsdp"),
            P("expert", "dp", "fsdp"),
            P("expert", "fsdp", "dp"),
            P("fsdp", ("expert", "dp"), None),
            P("fsdp", ("expert", "dp"), None),
        ),
        check_vma=False,
    )
```

```python
import functools

import jax
import jax.numpy as jnp
from jax import lax
from jax.experimental import pallas as pl
from jax.experimental.pallas import tpu as pltpu
from jax.sharding import PartitionSpec as P

BF = jnp.bfloat16
F32 = jnp.float32


def dot(a, b, ca, cb):
    return lax.dot_general(a, b, (((ca,), (cb,)), ((), ())), preferred_element_type=F32)


VMEM = pl.BlockSpec(memory_space=pltpu.VMEM)
SMEM = pl.BlockSpec(memory_space=pltpu.SMEM)


def call(kernel, shapes, in_specs, scratch=(), flops=0):
    return pl.pallas_call(
        kernel,
        out_shape=[jax.ShapeDtypeStruct(s, t) for s, t in shapes],
        in_specs=in_specs,
        out_specs=[VMEM] * len(shapes),
        scratch_shapes=scratch,
        cost_estimate=pl.CostEstimate(flops=flops, bytes_accessed=4 << 20, transcendentals=0),
        compiler_params=pltpu.CompilerParams(vmem_limit_bytes=40 << 20),
    )


def stack(a_ref, b_ref, a_rows, b_rows):
    a, b = a_ref[:, a_rows], b_ref[:, b_rows]
    return jnp.concatenate([a.reshape(-1, a.shape[2]), b.reshape(-1, b.shape[2])], axis=0)


def hidden_kernel(
    xa, yb, a_ref, b_ref, gate_ref, up_ref, down_ref, prob_ref,
    dx_ref, pair_ref, scaled_ref, score_ref,
):
    units = gate_ref.shape[1]
    x_t = stack(a_ref, b_ref, slice(0, xa), slice(yb, None))
    gate = dot(gate_ref[...], x_t, 0, 0)
    up = dot(up_ref[...], x_t, 0, 0)
    y_t = stack(a_ref, b_ref, slice(xa, None), slice(0, yb))
    back = dot(down_ref[...], y_t, 1, 0)
    prob = prob_ref[...]
    sig = jax.nn.sigmoid(gate)
    swish = gate * sig
    hidden = swish * up
    scaled_ref[...] = (prob * hidden).astype(BF)
    score_ref[...] = jnp.sum(hidden.astype(BF).astype(F32) * back, axis=0, keepdims=True)
    scaled_back = prob * back
    pair_ref[:units] = (scaled_back * up * sig * (1.0 + gate * (1.0 - sig))).astype(BF)
    pair_ref[units:] = (scaled_back * swish).astype(BF)
    pair = pair_ref[...]
    step = dx_ref.shape[0] // 8
    for i in range(8):
        at = slice(i * step, (i + 1) * step)
        both = jnp.concatenate([gate_ref[at], up_ref[at]], axis=1)
        dx_ref[at] = dot(both, pair, 1, 0).astype(BF)


def weight_kernel(xa, yb, core_ref, a_ref, b_ref, pair_ref, scaled_ref, away_ref, kept_ref, y_ref):
    units = scaled_ref.shape[0]
    y_ref[...] = stack(a_ref, b_ref, slice(xa, None), slice(0, yb))
    pair, scaled = pair_ref[...], scaled_ref[...]
    quarter = y_ref.shape[0] // 4
    lines = quarter // xa
    core = core_ref[0]
    for half in range(2):
        source, rows = (a_ref, slice(0, xa)) if half == 0 else (b_ref, slice(yb, None))
        for out_ref, which in ((away_ref, 1 - core), (kept_ref, core)):
            x_t = source[pl.ds(which * lines, lines), rows].reshape(quarter, -1)
            grads = dot(x_t, pair, 1, 1)
            out_ref[half, :quarter] = grads[:, :units].astype(BF)
            out_ref[half, quarter : 2 * quarter] = grads[:, units:].astype(BF)
            start = pl.multiple_of((2 * half + which) * quarter, quarter)
            down = dot(scaled, y_ref[pl.ds(start, quarter)], 1, 1).astype(BF)
            for q in range(quarter // units):
                at = 2 * quarter + q * units
                out_ref[half, at : at + units] = down[:, q * units : (q + 1) * units]


def return_kernel(feats, parts_ref, target_ref, score_ref, out_ref):
    own_dx = jnp.sum(parts_ref[...].astype(F32), axis=0).astype(BF)
    rows = own_dx.shape[1]
    owned = target_ref.shape[1]
    score = score_ref[...]
    high = score.astype(BF).astype(F32)
    low = score - high
    blank = jnp.zeros((feats, rows), BF)
    line = lax.broadcasted_iota(jnp.int32, (owned * feats, rows), 0)
    row = lax.broadcasted_iota(jnp.int32, (target_ref.shape[0], rows), 1)
    total = 0.0
    for j in range(owned):
        tail = jnp.where(line == 2 * j, high, jnp.where(line == 2 * j + 1, low, 0.0)).astype(BF)
        laid = [own_dx if i == j else blank for i in range(owned)] + [tail]
        pick = jnp.where(row == target_ref[:, j : j + 1], 1.0, 0.0).astype(BF)
        total = total + dot(pick, jnp.concatenate(laid, axis=0), 1, 1)
    out_ref[...] = total.astype(BF)


def sum_kernel(scores_ref, kept_ref, far_ref, gate_ref, up_ref, down_ref):
    del scores_ref
    quarter, units = gate_ref.shape[1:]
    total = (kept_ref[...] + far_ref[...].astype(F32)).astype(BF)
    gate_ref[0] = total[:quarter]
    up_ref[0] = total[quarter : 2 * quarter]
    for q in range(quarter // units):
        at = 2 * quarter + q * units
        down_ref[0, :, q * units : (q + 1) * units] = total[at : at + units]


def shards(
    tokens, cotangent, expert_ids, slot_ids, route_probs, gate_weight, up_weight, down_weight
):
    peers = lax.axis_size("fsdp")
    experts = lax.axis_size("expert")
    mine = lax.axis_index("expert")
    owned, _, width = tokens.shape
    feats = width // peers
    capacity = 2 * expert_ids.shape[0] // experts
    rows = experts * capacity
    units = gate_weight.shape[2]

    side = 1
    while side * side < peers:
        side *= 2
    xa, ya, xb, yb = feats * 4 * side // 8, feats * 3 * side // 8, feats * 4 * side // 8, feats * 5 * side // 8
    in_row = [[i * side + j for j in range(side)] for i in range(side)]
    in_column = [[i * side + j for i in range(side)] for j in range(side)]

    fields = [expert_ids[:, 0, :].astype(BF), slot_ids[:, 0, :].astype(BF), route_probs[:, 0, :]]
    fields = jnp.concatenate(fields, axis=1).reshape(peers, owned * 6)

    own_x, own_y = tokens[:, 0, :], cotangent[:, 0, :]
    full = (owned, side, side)
    a_x = own_x[:, : side * xa].reshape(owned, 1, side, xa)
    a_y = own_y[:, : side * ya].reshape(owned, 1, side, ya)
    b_y = own_y[:, side * ya :].reshape(owned, side, 1, yb)
    b_x = own_x[:, side * xa :].reshape(owned, side, 1, xb)
    cut = [jnp.broadcast_to(v, full + v.shape[3:]) for v in (a_x, a_y, b_y, b_x)]
    cut = jnp.concatenate(cut, axis=3).transpose(1, 2, 0, 3)
    part = xa + ya + xb + yb
    block = cut.reshape(peers, owned * part // 128, 128)
    block = jnp.broadcast_to(block[None], (experts,) + block.shape)
    block = block.reshape((experts * peers,) + block.shape[2:])
    got = lax.all_to_all(block, ("expert", "fsdp"), 0, 0, tiled=True)
    shifts = [fields] + [
        lax.ppermute(fields, "expert", [(i, (i + d) % experts) for i in range(experts)])
        for d in range(1, experts)
    ]
    turned = jnp.concatenate(shifts[::-1] + shifts[:0:-1], axis=0)
    got_route = lax.dynamic_slice_in_dim(
        turned, (experts - 1 - mine) * peers, experts * peers, 0
    ).astype(F32)
    got_cut = got.reshape(experts * peers, owned, part)

    source = lax.broadcasted_iota(jnp.int32, (peers * experts, 1), 0) // peers * capacity
    row_iota = lax.broadcasted_iota(jnp.int32, (peers * experts, rows), 1)
    targets, prob_row, cut_t = [], 0.0, 0.0
    for j in range(owned):
        first_at = 6 * j
        route = got_route[:, first_at : first_at + 6]
        first = jnp.logical_and(route[:, 0:1] == mine.astype(F32), route[:, 2:3] >= 0)
        second = jnp.logical_and(route[:, 1:2] == mine.astype(F32), route[:, 3:4] >= 0)
        slot = jnp.where(first, route[:, 2:3], route[:, 3:4]).astype(jnp.int32)
        target = jnp.where(jnp.logical_or(first, second), source + slot, -1)
        pick = row_iota == target
        prob = jnp.where(first, route[:, 4:5], route[:, 5:6])
        prob_row = prob_row + jnp.sum(jnp.where(pick, prob, 0.0), axis=0, keepdims=True)
        targets.append(target)
        cut_t = cut_t + dot(got_cut[:, j], pick.astype(BF), 0, 0)
    cut_t = cut_t.astype(BF)
    a_cut, b_cut = cut_t[: xa + ya], cut_t[xa + ya :]
    b_cut = jnp.broadcast_to(b_cut[None], (side,) + b_cut.shape)
    b_full = lax.all_to_all(b_cut, "fsdp", 0, 0, axis_index_groups=in_column, tiled=True)
    a_full = lax.all_gather(a_cut, "fsdp", axis=0, axis_index_groups=in_row)
    a_full, b_full = a_full.reshape(side, xa + ya, rows), b_full.reshape(side, xb + yb, rows)
    dx, pair, scaled, score = call(
        functools.partial(hidden_kernel, xa, yb),
        [((width, rows), BF), ((2 * units, rows), BF), ((units, rows), BF), ((1, rows), F32)],
        [VMEM] * 6,
        flops=10 * width * units * rows,
    )(a_full, b_full, gate_weight[0], up_weight[0], down_weight[0], prob_row)

    parts = lax.all_to_all(dx.reshape(peers, feats, rows), "fsdp", 0, 0, tiled=True)

    quarter = width // 4
    dp = lax.axis_index("dp")
    core, half = dp % 2, dp // 2
    away, kept = call(
        functools.partial(weight_kernel, xa, yb),
        [((2, 3 * quarter, units), BF)] * 2,
        [SMEM] + [VMEM] * 4,
        [pltpu.VMEM((width, rows), BF)],
        flops=6 * width * units * rows,
    )(core[None], a_full, b_full, pair, scaled)
    near = lax.ppermute(away, "dp", [(0, 1), (1, 0), (2, 3), (3, 2)])
    both = kept.astype(F32) + near.astype(F32)
    away = lax.dynamic_index_in_dim(both, 1 - half, 0, keepdims=False).astype(BF)
    kept = lax.dynamic_index_in_dim(both, half, 0, keepdims=False)
    far = lax.ppermute(away, "dp", [(0, 2), (2, 0), (1, 3), (3, 1)])

    (returned,) = call(
        functools.partial(return_kernel, feats),
        [((experts * peers, 2 * owned * feats), BF)],
        [VMEM] * 3,
    )(parts, jnp.concatenate(targets, axis=1), score)
    home = lax.all_to_all(returned, ("expert", "fsdp"), 0, 0, tiled=True)
    home = home.astype(F32).reshape(experts, peers, 2 * owned * feats)
    token_grad = jnp.sum(home[:, :, : owned * feats], axis=0).astype(BF)
    token_grad = token_grad.reshape(peers, owned, feats).transpose(1, 0, 2).reshape(owned, 1, width)
    scores = jnp.sum(home[:, :, owned * feats : owned * feats + 2 * owned], axis=1)
    scores = scores.reshape(experts, owned, 2).sum(axis=2)
    me = lax.axis_index("fsdp")
    own_ids = lax.dynamic_slice_in_dim(expert_ids[:, 0, :], me * owned, owned, 0)
    own_slots = lax.dynamic_slice_in_dim(slot_ids[:, 0, :], me * owned, owned, 0)
    expert_iota = lax.broadcasted_iota(jnp.int32, (experts, owned, 2), 0)
    chosen = jnp.logical_and(expert_iota == own_ids[None], own_slots[None] >= 0)
    prob_grad = jnp.sum(jnp.where(chosen, scores[:, :, None], 0.0), axis=0)
    grad_gate, grad_up, grad_down = call(
        sum_kernel,
        [((1, quarter, units), BF)] * 2 + [((1, units, quarter), BF)],
        [pl.BlockSpec(memory_space=pl.ANY)] + [VMEM] * 2,
    )(scores, kept, far)
    return grad_gate, grad_up, grad_down, token_grad, prob_grad[:, None, :]


def solution(mesh):
    return jax.shard_map(
        shards,
        mesh=mesh,
        in_specs=(
            P("fsdp", ("expert", "dp"), None),
            P("fsdp", ("expert", "dp"), None),
            P(None, ("expert", "dp"), None),
            P(None, ("expert", "dp"), None),
            P(None, ("expert", "dp"), None),
            P("expert", None, "fsdp"),
            P("expert", None, "fsdp"),
            P("expert", "fsdp", None),
        ),
        out_specs=(
            P("expert", "dp", "fsdp"),
            P("expert", "dp", "fsdp"),
            P("expert", "fsdp", "dp"),
            P("fsdp", ("expert", "dp"), None),
            P("fsdp", ("expert", "dp"), None),
        ),
        check_vma=False,
    )
```

```python
import functools

import jax
import jax.numpy as jnp
from jax import lax
from jax.experimental import pallas as pl
from jax.experimental.pallas import tpu as pltpu
from jax.sharding import PartitionSpec as P

BF = jnp.bfloat16
F32 = jnp.float32


def dot(a, b, ca, cb):
    return lax.dot_general(a, b, (((ca,), (cb,)), ((), ())), preferred_element_type=F32)


VMEM = pl.BlockSpec(memory_space=pltpu.VMEM)
SMEM = pl.BlockSpec(memory_space=pltpu.SMEM)


ANY = pl.BlockSpec(memory_space=pl.ANY)
HBM = pl.BlockSpec(memory_space=pltpu.HBM)


def call(kernel, shapes, in_specs, scratch=(), flops=0):
    return pl.pallas_call(
        kernel,
        out_shape=[jax.ShapeDtypeStruct(s, t) for s, t in shapes],
        in_specs=in_specs,
        out_specs=[VMEM] * len(shapes),
        scratch_shapes=scratch,
        cost_estimate=pl.CostEstimate(flops=flops, bytes_accessed=4 << 20, transcendentals=0),
        compiler_params=pltpu.CompilerParams(vmem_limit_bytes=40 << 20),
    )


def send_kernel(side, ya, yb, x_ref, y_ref, out_ref, block_ref, sems):
    x, y = x_ref[...].astype(F32), y_ref[...].astype(F32)
    owned, lanes = x.shape[0], block_ref.shape[2]
    lane = lax.broadcasted_iota(jnp.int32, (owned, lanes), 1)
    none = jnp.zeros((owned, lanes), F32)

    def tile(lines):
        return jnp.concatenate([v[t : t + 1] for t in range(owned) for v in lines], axis=0)

    by_x, by_z = [], []
    for i in range(side):
        head = jnp.where(lane < ya, y[:, i * ya : i * ya + lanes], 0.0)
        by_x.append(tile([x[:, i * lanes : (i + 1) * lanes], head, none, none]))
        at = side * ya + i * yb
        middle = jnp.where(lane >= ya, y[:, at - ya : at - ya + lanes], 0.0)
        last = y[:, at + lanes - ya : at + 2 * lanes - ya]
        at = (side + i) * lanes
        by_z.append(tile([none, middle, last, x[:, at : at + lanes]]))
    for i in range(side):
        for j in range(side):
            block_ref[i * side + j] = (by_z[i] + by_x[j]).astype(BF)
    copies = [
        pltpu.make_async_copy(block_ref, out_ref.at[k], sems.at[k]) for k in range(out_ref.shape[0])
    ]
    for copy in copies:
        copy.start()
    for copy in copies:
        copy.wait()


def lay_out(own_x, own_y, experts, side, ya, yb):
    shape = (side * side, own_x.shape[0] * 4, 128)
    return pl.pallas_call(
        functools.partial(send_kernel, side, ya, yb),
        out_shape=jax.ShapeDtypeStruct((experts,) + shape, BF),
        in_specs=[VMEM] * 2,
        out_specs=HBM,
        scratch_shapes=[pltpu.VMEM(shape, BF), pltpu.SemaphoreType.DMA((experts,))],
        compiler_params=pltpu.CompilerParams(vmem_limit_bytes=40 << 20),
    )(own_x, own_y)


def stack(a_ref, b_ref, a_rows, b_rows):
    a, b = a_ref[:, a_rows], b_ref[:, b_rows]
    return jnp.concatenate([a.reshape(-1, a.shape[2]), b.reshape(-1, b.shape[2])], axis=0)


def hidden_kernel(
    xa, yb, a_ref, b_ref, gate_ref, up_ref, down_ref, prob_ref,
    dx_ref, pair_ref, scaled_ref, score_ref,
):
    units = gate_ref.shape[1]
    x_t = stack(a_ref, b_ref, slice(0, xa), slice(yb, None))
    gate = dot(gate_ref[...], x_t, 0, 0)
    up = dot(up_ref[...], x_t, 0, 0)
    y_t = stack(a_ref, b_ref, slice(xa, None), slice(0, yb))
    back = dot(down_ref[...], y_t, 1, 0)
    prob = prob_ref[...]
    sig = jax.nn.sigmoid(gate)
    swish = gate * sig
    hidden = swish * up
    scaled_ref[...] = (prob * hidden).astype(BF)
    score_ref[...] = jnp.sum(hidden.astype(BF).astype(F32) * back, axis=0, keepdims=True)
    scaled_back = prob * back
    pair_ref[:units] = (scaled_back * up * sig * (1.0 + gate * (1.0 - sig))).astype(BF)
    pair_ref[units:] = (scaled_back * swish).astype(BF)
    pair = pair_ref[...]
    step = dx_ref.shape[0] // 8
    for i in range(8):
        at = slice(i * step, (i + 1) * step)
        both = jnp.concatenate([gate_ref[at], up_ref[at]], axis=1)
        dx_ref[at] = dot(both, pair, 1, 0).astype(BF)


def weight_kernel(xa, yb, core_ref, a_ref, b_ref, pair_ref, scaled_ref, away_ref, kept_ref, y_ref):
    units = scaled_ref.shape[0]
    y_ref[...] = stack(a_ref, b_ref, slice(xa, None), slice(0, yb))
    pair, scaled = pair_ref[...], scaled_ref[...]
    quarter = y_ref.shape[0] // 4
    lines = quarter // xa
    core = core_ref[0]
    for half in range(2):
        source, rows = (a_ref, slice(0, xa)) if half == 0 else (b_ref, slice(yb, None))
        for out_ref, which in ((away_ref, 1 - core), (kept_ref, core)):
            x_t = source[pl.ds(which * lines, lines), rows].reshape(quarter, -1)
            grads = dot(x_t, pair, 1, 1)
            out_ref[half, :quarter] = grads[:, :units].astype(BF)
            out_ref[half, quarter : 2 * quarter] = grads[:, units:].astype(BF)
            start = pl.multiple_of((2 * half + which) * quarter, quarter)
            down = dot(scaled, y_ref[pl.ds(start, quarter)], 1, 1).astype(BF)
            for q in range(quarter // units):
                at = 2 * quarter + q * units
                out_ref[half, at : at + units] = down[:, q * units : (q + 1) * units]


def return_kernel(feats, parts_ref, target_ref, score_ref, out_ref):
    own_dx = jnp.sum(parts_ref[...].astype(F32), axis=0).astype(BF)
    rows = own_dx.shape[1]
    owned = target_ref.shape[1]
    score = score_ref[...]
    high = score.astype(BF).astype(F32)
    low = score - high
    blank = jnp.zeros((feats, rows), BF)
    line = lax.broadcasted_iota(jnp.int32, (owned * feats, rows), 0)
    row = lax.broadcasted_iota(jnp.int32, (target_ref.shape[0], rows), 1)
    total = 0.0
    for j in range(owned):
        tail = jnp.where(line == 2 * j, high, jnp.where(line == 2 * j + 1, low, 0.0)).astype(BF)
        laid = [own_dx if i == j else blank for i in range(owned)] + [tail]
        pick = jnp.where(row == target_ref[:, j : j + 1], 1.0, 0.0).astype(BF)
        total = total + dot(pick, jnp.concatenate(laid, axis=0), 1, 1)
    out_ref[...] = total.astype(BF)


def sum_kernel(scores_ref, kept_ref, far_ref, gate_ref, up_ref, down_ref):
    del scores_ref
    quarter, units = gate_ref.shape[1:]
    total = (kept_ref[...] + far_ref[...].astype(F32)).astype(BF)
    gate_ref[0] = total[:quarter]
    up_ref[0] = total[quarter : 2 * quarter]
    for q in range(quarter // units):
        at = 2 * quarter + q * units
        down_ref[0, :, q * units : (q + 1) * units] = total[at : at + units]


def shards(
    tokens, cotangent, expert_ids, slot_ids, route_probs, gate_weight, up_weight, down_weight
):
    peers = lax.axis_size("fsdp")
    experts = lax.axis_size("expert")
    mine = lax.axis_index("expert")
    owned, _, width = tokens.shape
    feats = width // peers
    capacity = 2 * expert_ids.shape[0] // experts
    rows = experts * capacity
    units = gate_weight.shape[2]

    side = 1
    while side * side < peers:
        side *= 2
    xa = xb = feats * side // 2
    ya, yb = feats * side * 7 // 16, feats * side * 9 // 16
    in_row = [[i * side + j for j in range(side)] for i in range(side)]
    in_column = [[i * side + j for i in range(side)] for j in range(side)]

    fields = [expert_ids[:, 0, :].astype(BF), slot_ids[:, 0, :].astype(BF), route_probs[:, 0, :]]
    fields = jnp.concatenate(fields, axis=1).reshape(peers, owned * 6)

    part = xa + ya + xb + yb
    block = lay_out(tokens[:, 0, :], cotangent[:, 0, :], experts, side, ya, yb)
    block = block.reshape((experts * peers,) + block.shape[2:])
    got = lax.all_to_all(block, ("expert", "fsdp"), 0, 0, tiled=True)
    shifts = [fields] + [
        lax.ppermute(fields, "expert", [(i, (i + d) % experts) for i in range(experts)])
        for d in range(1, experts)
    ]
    turned = jnp.concatenate(shifts[::-1] + shifts[:0:-1], axis=0)
    got_route = lax.dynamic_slice_in_dim(
        turned, (experts - 1 - mine) * peers, experts * peers, 0
    ).astype(F32)
    got_cut = got.reshape(experts * peers, owned, part)

    source = lax.broadcasted_iota(jnp.int32, (peers * experts, 1), 0) // peers * capacity
    row_iota = lax.broadcasted_iota(jnp.int32, (peers * experts, rows), 1)
    targets, prob_row, cut_t = [], 0.0, 0.0
    for j in range(owned):
        first_at = 6 * j
        route = got_route[:, first_at : first_at + 6]
        first = jnp.logical_and(route[:, 0:1] == mine.astype(F32), route[:, 2:3] >= 0)
        second = jnp.logical_and(route[:, 1:2] == mine.astype(F32), route[:, 3:4] >= 0)
        slot = jnp.where(first, route[:, 2:3], route[:, 3:4]).astype(jnp.int32)
        target = jnp.where(jnp.logical_or(first, second), source + slot, -1)
        pick = row_iota == target
        prob = jnp.where(first, route[:, 4:5], route[:, 5:6])
        prob_row = prob_row + jnp.sum(jnp.where(pick, prob, 0.0), axis=0, keepdims=True)
        targets.append(target)
        cut_t = cut_t + dot(got_cut[:, j], pick.astype(BF), 0, 0)
    cut_t = cut_t.astype(BF)
    a_cut, b_cut = cut_t[: xa + ya], cut_t[xa + ya :]
    b_cut = jnp.broadcast_to(b_cut[None], (side,) + b_cut.shape)
    b_full = lax.all_to_all(b_cut, "fsdp", 0, 0, axis_index_groups=in_column, tiled=True)
    a_full = lax.all_gather(a_cut, "fsdp", axis=0, axis_index_groups=in_row)
    a_full, b_full = a_full.reshape(side, xa + ya, rows), b_full.reshape(side, xb + yb, rows)
    dx, pair, scaled, score = call(
        functools.partial(hidden_kernel, xa, yb),
        [((width, rows), BF), ((2 * units, rows), BF), ((units, rows), BF), ((1, rows), F32)],
        [VMEM] * 6,
        flops=10 * width * units * rows,
    )(a_full, b_full, gate_weight[0], up_weight[0], down_weight[0], prob_row)

    parts = lax.all_to_all(dx.reshape(peers, feats, rows), "fsdp", 0, 0, tiled=True)

    quarter = width // 4
    dp = lax.axis_index("dp")
    core, half = dp % 2, dp // 2
    away, kept = call(
        functools.partial(weight_kernel, xa, yb),
        [((2, 3 * quarter, units), BF)] * 2,
        [SMEM] + [VMEM] * 4,
        [pltpu.VMEM((width, rows), BF)],
        flops=6 * width * units * rows,
    )(core[None], a_full, b_full, pair, scaled)
    near = lax.ppermute(away, "dp", [(0, 1), (1, 0), (2, 3), (3, 2)])
    both = kept.astype(F32) + near.astype(F32)
    away = lax.dynamic_index_in_dim(both, 1 - half, 0, keepdims=False).astype(BF)
    kept = lax.dynamic_index_in_dim(both, half, 0, keepdims=False)
    far = lax.ppermute(away, "dp", [(0, 2), (2, 0), (1, 3), (3, 1)])

    (returned,) = call(
        functools.partial(return_kernel, feats),
        [((experts * peers, 2 * owned * feats), BF)],
        [VMEM] * 3,
    )(parts, jnp.concatenate(targets, axis=1), score)
    home = lax.all_to_all(returned, ("expert", "fsdp"), 0, 0, tiled=True)
    home = home.astype(F32).reshape(experts, peers, 2 * owned * feats)
    token_grad = jnp.sum(home[:, :, : owned * feats], axis=0).astype(BF)
    token_grad = token_grad.reshape(peers, owned, feats).transpose(1, 0, 2).reshape(owned, 1, width)
    scores = jnp.sum(home[:, :, owned * feats : owned * feats + 2 * owned], axis=1)
    scores = scores.reshape(experts, owned, 2).sum(axis=2)
    me = lax.axis_index("fsdp")
    own_ids = lax.dynamic_slice_in_dim(expert_ids[:, 0, :], me * owned, owned, 0)
    own_slots = lax.dynamic_slice_in_dim(slot_ids[:, 0, :], me * owned, owned, 0)
    expert_iota = lax.broadcasted_iota(jnp.int32, (experts, owned, 2), 0)
    chosen = jnp.logical_and(expert_iota == own_ids[None], own_slots[None] >= 0)
    prob_grad = jnp.sum(jnp.where(chosen, scores[:, :, None], 0.0), axis=0)
    grad_gate, grad_up, grad_down = call(
        sum_kernel,
        [((1, quarter, units), BF)] * 2 + [((1, units, quarter), BF)],
        [ANY] + [VMEM] * 2,
    )(scores, kept, far)
    return grad_gate, grad_up, grad_down, token_grad, prob_grad[:, None, :]


def solution(mesh):
    return jax.shard_map(
        shards,
        mesh=mesh,
        in_specs=(
            P("fsdp", ("expert", "dp"), None),
            P("fsdp", ("expert", "dp"), None),
            P(None, ("expert", "dp"), None),
            P(None, ("expert", "dp"), None),
            P(None, ("expert", "dp"), None),
            P("expert", None, "fsdp"),
            P("expert", None, "fsdp"),
            P("expert", "fsdp", None),
        ),
        out_specs=(
            P("expert", "dp", "fsdp"),
            P("expert", "dp", "fsdp"),
            P("expert", "fsdp", "dp"),
            P("fsdp", ("expert", "dp"), None),
            P("fsdp", ("expert", "dp"), None),
        ),
        check_vma=False,
    )
```

```python
import functools

import jax
import jax.numpy as jnp
from jax import lax
from jax.experimental import pallas as pl
from jax.experimental.pallas import tpu as pltpu
from jax.sharding import PartitionSpec as P

BF = jnp.bfloat16
F32 = jnp.float32


def dot(a, b, ca, cb):
    return lax.dot_general(a, b, (((ca,), (cb,)), ((), ())), preferred_element_type=F32)


VMEM = pl.BlockSpec(memory_space=pltpu.VMEM)
SMEM = pl.BlockSpec(memory_space=pltpu.SMEM)


ANY = pl.BlockSpec(memory_space=pl.ANY)
HBM = pl.BlockSpec(memory_space=pltpu.HBM)


def call(kernel, shapes, in_specs, scratch=(), flops=0):
    return pl.pallas_call(
        kernel,
        out_shape=[jax.ShapeDtypeStruct(s, t) for s, t in shapes],
        in_specs=in_specs,
        out_specs=[VMEM] * len(shapes),
        scratch_shapes=scratch,
        cost_estimate=pl.CostEstimate(flops=flops, bytes_accessed=4 << 20, transcendentals=0),
        compiler_params=pltpu.CompilerParams(vmem_limit_bytes=40 << 20),
    )


def send_kernel(side, ya, yb, x_ref, y_ref, out_ref, block_ref, sems):
    x, y = x_ref[...].astype(F32), y_ref[...].astype(F32)
    owned, lanes = x.shape[0], block_ref.shape[2]
    lane = lax.broadcasted_iota(jnp.int32, (owned, lanes), 1)
    none = jnp.zeros((owned, lanes), F32)

    def tile(lines):
        return jnp.concatenate([v[t : t + 1] for t in range(owned) for v in lines], axis=0)

    by_x, by_z = [], []
    for i in range(side):
        head = jnp.where(lane < ya, y[:, i * ya : i * ya + lanes], 0.0)
        by_x.append(tile([x[:, i * lanes : (i + 1) * lanes], head, none, none]))
        at = side * ya + i * yb
        middle = jnp.where(lane >= ya, y[:, at - ya : at - ya + lanes], 0.0)
        last = y[:, at + lanes - ya : at + 2 * lanes - ya]
        at = (side + i) * lanes
        by_z.append(tile([none, middle, last, x[:, at : at + lanes]]))
    for i in range(side):
        for j in range(side):
            block_ref[i * side + j] = (by_z[i] + by_x[j]).astype(BF)
    copies = [
        pltpu.make_async_copy(block_ref, out_ref.at[k], sems.at[k]) for k in range(out_ref.shape[0])
    ]
    for copy in copies:
        copy.start()
    for copy in copies:
        copy.wait()


def lay_out(own_x, own_y, experts, side, ya, yb):
    shape = (side * side, own_x.shape[0] * 4, 128)
    return pl.pallas_call(
        functools.partial(send_kernel, side, ya, yb),
        out_shape=jax.ShapeDtypeStruct((experts,) + shape, BF),
        in_specs=[VMEM] * 2,
        out_specs=HBM,
        scratch_shapes=[pltpu.VMEM(shape, BF), pltpu.SemaphoreType.DMA((experts,))],
        compiler_params=pltpu.CompilerParams(vmem_limit_bytes=60 << 20),
    )(own_x, own_y)


def stack(a_ref, b_ref, a_rows, b_rows):
    a, b = a_ref[:, a_rows], b_ref[:, b_rows]
    return jnp.concatenate([a.reshape(-1, a.shape[2]), b.reshape(-1, b.shape[2])], axis=0)


def hidden_kernel(
    xa, yb, a_ref, b_ref, gate_ref, up_ref, down_ref, prob_ref,
    dx_ref, pair_ref, scaled_ref, score_ref,
):
    units = gate_ref.shape[1]
    x_t = stack(a_ref, b_ref, slice(0, xa), slice(yb, None))
    gate = dot(gate_ref[...], x_t, 0, 0)
    up = dot(up_ref[...], x_t, 0, 0)
    y_t = stack(a_ref, b_ref, slice(xa, None), slice(0, yb))
    back = dot(down_ref[...], y_t, 1, 0)
    prob = prob_ref[...]
    sig = jax.nn.sigmoid(gate)
    swish = gate * sig
    hidden = swish * up
    scaled_ref[...] = (prob * hidden).astype(BF)
    score_ref[...] = jnp.sum(hidden.astype(BF).astype(F32) * back, axis=0, keepdims=True)
    scaled_back = prob * back
    pair_ref[:units] = (scaled_back * up * sig * (1.0 + gate * (1.0 - sig))).astype(BF)
    pair_ref[units:] = (scaled_back * swish).astype(BF)
    pair = pair_ref[...]
    step = dx_ref.shape[0] // 8
    for i in range(8):
        at = slice(i * step, (i + 1) * step)
        both = jnp.concatenate([gate_ref[at], up_ref[at]], axis=1)
        dx_ref[at] = dot(both, pair, 1, 0).astype(BF)


def weight_kernel(xa, yb, core_ref, a_ref, b_ref, pair_ref, scaled_ref, away_ref, kept_ref, y_ref):
    units = scaled_ref.shape[0]
    y_ref[...] = stack(a_ref, b_ref, slice(xa, None), slice(0, yb))
    pair, scaled = pair_ref[...], scaled_ref[...]
    quarter = y_ref.shape[0] // 4
    lines = quarter // xa
    core = core_ref[0]
    for half in range(2):
        source, rows = (a_ref, slice(0, xa)) if half == 0 else (b_ref, slice(yb, None))
        for out_ref, which in ((away_ref, 1 - core), (kept_ref, core)):
            x_t = source[pl.ds(which * lines, lines), rows].reshape(quarter, -1)
            grads = dot(x_t, pair, 1, 1)
            out_ref[half, :quarter] = grads[:, :units].astype(BF)
            out_ref[half, quarter : 2 * quarter] = grads[:, units:].astype(BF)
            start = pl.multiple_of((2 * half + which) * quarter, quarter)
            down = dot(scaled, y_ref[pl.ds(start, quarter)], 1, 1).astype(BF)
            for q in range(quarter // units):
                at = 2 * quarter + q * units
                out_ref[half, at : at + units] = down[:, q * units : (q + 1) * units]


def return_kernel(feats, parts_ref, target_ref, score_ref, out_ref):
    own_dx = jnp.sum(parts_ref[...].astype(F32), axis=0).astype(BF)
    rows = own_dx.shape[1]
    owned = target_ref.shape[1]
    score = score_ref[...]
    high = score.astype(BF).astype(F32)
    low = score - high
    blank = jnp.zeros((feats, rows), BF)
    line = lax.broadcasted_iota(jnp.int32, (owned * feats, rows), 0)
    row = lax.broadcasted_iota(jnp.int32, (target_ref.shape[0], rows), 1)
    total = 0.0
    for j in range(owned):
        tail = jnp.where(line == 2 * j, high, jnp.where(line == 2 * j + 1, low, 0.0)).astype(BF)
        laid = [own_dx if i == j else blank for i in range(owned)] + [tail]
        pick = jnp.where(row == target_ref[:, j : j + 1], 1.0, 0.0).astype(BF)
        total = total + dot(pick, jnp.concatenate(laid, axis=0), 1, 1)
    out_ref[...] = total.astype(BF)


def sum_kernel(sent_ref, kept_ref, far_ref, gate_ref, up_ref, down_ref):
    del sent_ref
    quarter, units = gate_ref.shape[1:]
    total = (kept_ref[...] + far_ref[...].astype(F32)).astype(BF)
    gate_ref[0] = total[:quarter]
    up_ref[0] = total[quarter : 2 * quarter]
    for q in range(quarter // units):
        at = 2 * quarter + q * units
        down_ref[0, :, q * units : (q + 1) * units] = total[at : at + units]


def shards(
    tokens, cotangent, expert_ids, slot_ids, route_probs, gate_weight, up_weight, down_weight
):
    peers = lax.axis_size("fsdp")
    experts = lax.axis_size("expert")
    mine = lax.axis_index("expert")
    owned, _, width = tokens.shape
    feats = width // peers
    capacity = 2 * expert_ids.shape[0] // experts
    rows = experts * capacity
    units = gate_weight.shape[2]

    side = 1
    while side * side < peers:
        side *= 2
    xa = xb = feats * side // 2
    ya, yb = feats * side * 7 // 16, feats * side * 9 // 16
    in_row = [[i * side + j for j in range(side)] for i in range(side)]
    in_column = [[i * side + j for i in range(side)] for j in range(side)]

    fields = [expert_ids[:, 0, :].astype(BF), slot_ids[:, 0, :].astype(BF), route_probs[:, 0, :]]
    fields = jnp.concatenate(fields, axis=1).reshape(peers, owned * 6)

    part = xa + ya + xb + yb
    block = lay_out(tokens[:, 0, :], cotangent[:, 0, :], experts, side, ya, yb)
    block = block.reshape((experts * peers,) + block.shape[2:])
    got = lax.all_to_all(block, ("expert", "fsdp"), 0, 0, tiled=True)
    shifts = [fields] + [
        lax.ppermute(fields, "expert", [(i, (i + d) % experts) for i in range(experts)])
        for d in range(1, experts)
    ]
    turned = jnp.concatenate(shifts[::-1] + shifts[:0:-1], axis=0)
    got_route = lax.dynamic_slice_in_dim(
        turned, (experts - 1 - mine) * peers, experts * peers, 0
    ).astype(F32)
    got_cut = got.reshape(experts * peers, owned, part)

    source = lax.broadcasted_iota(jnp.int32, (peers * experts, 1), 0) // peers * capacity
    row_iota = lax.broadcasted_iota(jnp.int32, (peers * experts, rows), 1)
    targets, prob_row, cut_t = [], 0.0, 0.0
    for j in range(owned):
        first_at = 6 * j
        route = got_route[:, first_at : first_at + 6]
        first = jnp.logical_and(route[:, 0:1] == mine.astype(F32), route[:, 2:3] >= 0)
        second = jnp.logical_and(route[:, 1:2] == mine.astype(F32), route[:, 3:4] >= 0)
        slot = jnp.where(first, route[:, 2:3], route[:, 3:4]).astype(jnp.int32)
        target = jnp.where(jnp.logical_or(first, second), source + slot, -1)
        pick = row_iota == target
        prob = jnp.where(first, route[:, 4:5], route[:, 5:6])
        prob_row = prob_row + jnp.sum(jnp.where(pick, prob, 0.0), axis=0, keepdims=True)
        targets.append(target)
        cut_t = cut_t + dot(got_cut[:, j], pick.astype(BF), 0, 0)
    cut_t = cut_t.astype(BF)
    a_cut, b_cut = cut_t[: xa + ya], cut_t[xa + ya :]
    b_cut = jnp.broadcast_to(b_cut[None], (side,) + b_cut.shape)
    b_full = lax.all_to_all(b_cut, "fsdp", 0, 0, axis_index_groups=in_column, tiled=True)
    a_full = lax.all_gather(a_cut, "fsdp", axis=0, axis_index_groups=in_row)
    a_full, b_full = a_full.reshape(side, xa + ya, rows), b_full.reshape(side, xb + yb, rows)
    dx, pair, scaled, score = call(
        functools.partial(hidden_kernel, xa, yb),
        [((width, rows), BF), ((2 * units, rows), BF), ((units, rows), BF), ((1, rows), F32)],
        [VMEM] * 6,
        flops=10 * width * units * rows,
    )(a_full, b_full, gate_weight[0], up_weight[0], down_weight[0], prob_row)

    parts = lax.all_to_all(dx.reshape(peers, feats, rows), "fsdp", 0, 0, tiled=True)

    quarter = width // 4
    dp = lax.axis_index("dp")
    core, half = dp % 2, dp // 2
    away, kept = call(
        functools.partial(weight_kernel, xa, yb),
        [((2, 3 * quarter, units), BF)] * 2,
        [SMEM] + [VMEM] * 4,
        [pltpu.VMEM((width, rows), BF)],
        flops=6 * width * units * rows,
    )(core[None], a_full, b_full, pair, scaled)
    near = lax.ppermute(away, "dp", [(0, 1), (1, 0), (2, 3), (3, 2)])
    both = kept.astype(F32) + near.astype(F32)
    away = lax.dynamic_index_in_dim(both, 1 - half, 0, keepdims=False).astype(BF)
    kept = lax.dynamic_index_in_dim(both, half, 0, keepdims=False)
    far = lax.ppermute(away, "dp", [(0, 2), (2, 0), (1, 3), (3, 1)])

    (returned,) = call(
        functools.partial(return_kernel, feats),
        [((experts * peers, 2 * owned * feats), BF)],
        [VMEM] * 3,
    )(parts, jnp.concatenate(targets, axis=1), score)
    home = lax.all_to_all(returned, ("expert", "fsdp"), 0, 0, tiled=True)
    home = home.astype(F32).reshape(experts, peers, 2 * owned * feats)
    token_grad = jnp.sum(home[:, :, : owned * feats], axis=0).astype(BF)
    token_grad = token_grad.reshape(peers, owned, feats).transpose(1, 0, 2).reshape(owned, 1, width)
    scores = jnp.sum(home[:, :, owned * feats : owned * feats + 2 * owned], axis=1)
    scores = scores.reshape(experts, owned, 2).sum(axis=2)
    me = lax.axis_index("fsdp")
    own_ids = lax.dynamic_slice_in_dim(expert_ids[:, 0, :], me * owned, owned, 0)
    own_slots = lax.dynamic_slice_in_dim(slot_ids[:, 0, :], me * owned, owned, 0)
    expert_iota = lax.broadcasted_iota(jnp.int32, (experts, owned, 2), 0)
    chosen = jnp.logical_and(expert_iota == own_ids[None], own_slots[None] >= 0)
    prob_grad = jnp.sum(jnp.where(chosen, scores[:, :, None], 0.0), axis=0)
    grad_gate, grad_up, grad_down = call(
        sum_kernel,
        [((1, quarter, units), BF)] * 2 + [((1, units, quarter), BF)],
        [ANY] + [VMEM] * 2,
    )(returned, kept, far)
    return grad_gate, grad_up, grad_down, token_grad, prob_grad[:, None, :]


def solution(mesh):
    return jax.shard_map(
        shards,
        mesh=mesh,
        in_specs=(
            P("fsdp", ("expert", "dp"), None),
            P("fsdp", ("expert", "dp"), None),
            P(None, ("expert", "dp"), None),
            P(None, ("expert", "dp"), None),
            P(None, ("expert", "dp"), None),
            P("expert", None, "fsdp"),
            P("expert", None, "fsdp"),
            P("expert", "fsdp", None),
        ),
        out_specs=(
            P("expert", "dp", "fsdp"),
            P("expert", "dp", "fsdp"),
            P("expert", "fsdp", "dp"),
            P("fsdp", ("expert", "dp"), None),
            P("fsdp", ("expert", "dp"), None),
        ),
        check_vma=False,
    )
```
